32 devices in a mesh: gx: 2 (over y), gy: 4 (over x, core), gz: 4 (over z).
Axes of the slice: x: 2, y: 2, z: 4, core: 2. Of those that a mesh axis runs over, the one named last changes fastest.
Arguments:
- features: bfloat16 [2, 16, 128, 256], P('gx', 'gy', 'gz'), may hold values from -6 to 6
- neighbour_code: int32 [2, 16, 128, 64], P('gx', 'gy', 'gz'), may hold values from 0 to 107, as said below
- distance: float32 [2, 16, 128, 64], P('gx', 'gy', 'gz'), may hold values from 0.8 to 4.8
- w_message: bfloat16 [2, 2048, 256], replicated, may hold values from -0.125 to 0.125
- w_update: bfloat16 [2, 256, 256], replicated, may hold values from -0.375 to 0.375
- norm_gain: float32 [2, 256], replicated, may hold values from 0.1 to 1.9
- w_env: bfloat16 [256, 128], replicated, may hold values from -0.375 to 0.375
- w_out: bfloat16 [3, 256], replicated, may hold values from -0.375 to 0.375
- w_first: bfloat16 [8, 128, 1024], P(('gx', 'gy')), may hold values from -0.5 to 0.5
- w_head: bfloat16 [8, 3, 1024], P(('gx', 'gy')), may hold values from -0.75 to 0.75
- flag_ids: int32 [2, 4, 4, 32], P('gx', 'gy', 'gz'), may hold values from 0 to 127, as said below
- flag_owner: int32 [2, 4, 4, 32, 1], P('gx', 'gy', 'gz'), may hold values from 0 to 7; in each aligned block of 32 rows (0 to 31, 32 to 63, ..., all dimensions but the last counted through in order) at most 8 rows name the same one
- flag_count: int32 [2, 4, 4], P('gx', 'gy', 'gz'), may hold values from 24 to 32, as said below
Outputs:
- forces: float32 [3, 2, 16, 128], P(None, 'gx', 'gy', 'gz')
The draws below stay inside these ranges and needn't reach their ends.
Inputs may be any that keep to these rules, and one draw needn't show every extreme that they name: `neighbour_code`: an atom's 64 codes are distinct and never name the atom itself (code 13 * 4 + its position along the thickness mod 4). `flag_ids`: the 32 indices of one device are distinct. `flag_owner`: of the 32 rows of one device, live or not, at most 8 name the same specialist, and some device has 8 rows naming one. Rows 0 to flag_count - 1 of a device are live; some device has all 32 live.
All inputs are finite; a program needn't handle non-finite values.
Results may differ from the reference program's by a relative error of at most 0.0085.
Values may be sent and summed in bfloat16 or wider, within the bound.
A program may use at most 64 MiB of HBM per device.

```python
import math
import jax
import jax.numpy as jnp
import numpy as np
from jax import lax

CX = 1
CY = 4
CZ = 8
M = 4
K = 64
F = 256
NRB = 8
L = 2
E = 128
HF = 1024
FLAG_DEV = 32
NOWN = 8
CAP = 8
NX = 2
NY = 16
ZM = 128
ATOMS_DEV = 128
N_GX = 2
N_GY = 4
N_GZ = 4


def draw_neighbour_code(key, part):
    candidates = 27 * M
    scores = jax.random.randint(key, (NX, NY, ZM, candidates), 0, 1 << 20) * candidates + jnp.arange(candidates, dtype=jnp.int32)
    self_code = 13 * M + jnp.arange(ZM, dtype=jnp.int32) % M
    scores = jnp.where(jnp.arange(candidates, dtype=jnp.int32)[None, None, None, :] == self_code[None, None, :, None], -1, scores)
    return lax.top_k(scores, K)[1].astype(jnp.int32)


def draw_flag_ids(key, part):
    device_keys = jax.random.split(key, N_GX * N_GY * N_GZ)
    chosen = jax.vmap(lambda single: jax.random.permutation(single, ATOMS_DEV)[:FLAG_DEV])(device_keys)
    return chosen.reshape(N_GX, N_GY, N_GZ, FLAG_DEV).astype(jnp.int32)


def draw_flag_count(key, part):
    counts = jax.random.randint(key, (N_GX, N_GY, N_GZ), 3 * FLAG_DEV // 4, FLAG_DEV + 1)
    return jnp.where(counts == jnp.max(counts), FLAG_DEV, counts).astype(jnp.int32)


def block_levels(own_key, extent, pieces, least, top_value):
    def one(dim, blocks):
        heights = jax.random.uniform(jax.random.fold_in(jax.random.fold_in(own_key, 6), dim), (blocks,), jnp.float32, least / len(pieces), top_value / len(pieces))
        return jnp.repeat(jnp.exp(heights), extent[dim] // blocks).reshape((-1,) + (1,) * (len(extent) - dim - 1))

    level = one(*pieces[0])
    for cut in pieces[1:]:
        level = level * one(*cut)
    return level


def shared_out(own_key, own, number, rows, number_of, top, limit, skew):
    ranking = jax.random.permutation(own_key, number_of)
    heavy_load, usual = load_shares(number_of, rows * top, limit, skew, True), load_shares(number_of, rows * top, limit, skew, False)
    places = jnp.arange(number_of)

    def named(tallies, offset_by):
        used = int((tallies > 0).sum())
        fixed = max(1, used // 4)
        shifted = fixed + (places - fixed + offset_by * (used - fixed)) % max(1, number_of - fixed)
        return jnp.zeros((number_of,), jnp.int32).at[ranking[jnp.where(places < fixed, places, shifted)]].set(jnp.asarray(tallies, jnp.int32))

    tallies = jnp.where(number % 4 == 0, named(heavy_load, number // 4), named(usual, number - number // 4 - 1))
    mixed = jax.random.permutation(jax.random.fold_in(own, 3), number_of)
    donor, sink = mixed[0:number_of // 2 * 2:2], mixed[1:number_of // 2 * 2:2]
    slack = jnp.minimum(tallies[donor] - 1, limit - tallies[sink]) // 2
    slack = jnp.where((donor == ranking[0]) | (sink == ranking[0]) | (tallies[sink] == 0), 0, jnp.maximum(slack, 0))
    shifted = jax.random.randint(jax.random.fold_in(own, 4), (number_of // 2,), 0, 1 << 20) % (slack + 1)
    tallies = tallies.at[donor].add(-shifted).at[sink].add(shifted)
    items = jnp.searchsorted(jnp.cumsum(tallies), jnp.arange(rows * top), side="right").astype(jnp.int32)
    listing = items.reshape(top, rows).T
    listing = listing[jax.random.permutation(jax.random.fold_in(own, 1), rows)]
    offset_by = jax.random.randint(jax.random.fold_in(own, 2), (rows, 1), 0, top)
    return jnp.take_along_axis(listing, (jnp.arange(top)[None, :] + offset_by) % top, axis=1)


def load_shares(count, total, most, skew, full):
    loads = [(1 << 20) // math.isqrt(rank ** skew) + 1 for rank in range(1, count + 1)]
    largest = most if full else min(most, max(-(-total // count), total * loads[0] // sum(loads)))
    least = 1 if total - largest >= count - 1 else 0
    given, rest = [largest] + [least] * (count - 1), total - largest - least * (count - 1)
    while rest > 0:
        free = [i for i in range(1, count) if given[i] < largest] or [i for i in range(1, count) if given[i] < most]
        whole, left = sum([loads[i] for i in free]), rest
        for i in free:
            more = min(most - given[i], max(1, left * loads[i] // whole), rest)
            given[i] = given[i] + more
            rest = rest - more
    return np.array(given)


def scatter_about(rng, extent, width, reach, shards=(), held_as=jnp.bfloat16):
    array = width * jax.random.normal(rng, extent, jnp.float32)
    if shards:
        array = array * block_levels(rng, extent, shards, -0.22, 0.18)
    return jnp.clip(array, -reach, reach).astype(held_as)


def setup_inputs(seed: int = 0) -> dict:
    keys = jax.random.split(jax.random.key(seed), 14)
    features = scatter_about(keys[0], (NX, NY, ZM, F), 1.0, 6.0, ((0, 2), (1, 4), (2, 4)))
    neighbour_code = draw_neighbour_code(jax.random.fold_in(keys[13], 71), 0)
    distance = jnp.clip(0.8 + 4 * jax.random.uniform(keys[2], (NX, NY, ZM, K), jnp.float32) ** block_levels(keys[2], (NX, NY, ZM, K), ((0, 2), (1, 4), (2, 4)), -0.2, 0.2), 0.8, 4.8)
    w_message = scatter_about(keys[3], (L, NRB * F, F), (NRB * F) ** -0.5, 0.125)
    w_update = scatter_about(keys[4], (L, F, F), F ** -0.5, 0.375)
    norm_gain = jnp.clip(1.0 + 0.18 * jax.random.normal(keys[5], (L, F), jnp.float32), 0.1, 1.9)
    w_env = scatter_about(keys[6], (F, E), F ** -0.5, 0.375)
    w_out = scatter_about(keys[7], (3, F), F ** -0.5, 0.375)
    w_first = scatter_about(keys[8], (NOWN, E, HF), E ** -0.5, 0.5, ((0, 8),))
    w_head = scatter_about(keys[9], (NOWN, 3, HF), 0.125, 0.75, ((0, 8),))
    flag_ids = draw_flag_ids(jax.random.fold_in(keys[13], 71), 0)
    flag_owner_keys = jax.random.split(jax.random.fold_in(keys[11], 1), N_GX * N_GY * N_GZ * FLAG_DEV // FLAG_DEV)
    flag_owner_turns = jax.random.permutation(jax.random.fold_in(keys[11], 3), N_GX * N_GY * N_GZ * FLAG_DEV // FLAG_DEV)
    flag_owner = jax.vmap(lambda own, number: shared_out(jax.random.fold_in(keys[11], 2), own, number, FLAG_DEV, NOWN, 1, CAP, 2))(flag_owner_keys, flag_owner_turns).reshape((N_GX, N_GY, N_GZ, FLAG_DEV, 1))
    flag_count = draw_flag_count(jax.random.fold_in(keys[13], 71), 0)
    return dict(features=features, neighbour_code=neighbour_code, distance=distance, w_message=w_message, w_update=w_update, norm_gain=norm_gain, w_env=w_env, w_out=w_out, w_first=w_first, w_head=w_head, flag_ids=flag_ids, flag_owner=flag_owner, flag_count=flag_count)


CUTOFF_RADIUS = 5.0
WIDTH_GAMMA = 2.0

def radial(distance):
    cutoff = 0.5 * (jnp.cos(jnp.pi * distance / CUTOFF_RADIUS) + 1.0)
    centres = 0.8 + jnp.arange(NRB).astype(distance.dtype) * (4.0 / (NRB - 1))
    radial_basis = jnp.exp(-WIDTH_GAMMA * (distance[..., None] - centres) ** 2) * cutoff[..., None]
    return (radial_basis.astype(jnp.bfloat16), cutoff)

def neighbour_rows(codes, coord_x, coord_y, coord_z, span_y, span_z):
    offset = codes // M
    within = codes % M
    step_x = offset // 9 - 1
    step_y = offset // 3 % 3 - 1
    step_z = offset % 3 - 1
    return ((coord_x + 1 + step_x) * span_y + (coord_y + 1 + step_y)) * span_z + (coord_z // M + 1 + step_z) * M + within

def update(state, summed, w_message, w_update, gain):
    message = jnp.dot(summed, w_message, preferred_element_type=jnp.float32)
    active = jax.nn.silu(message).astype(jnp.bfloat16)
    residual = state.astype(jnp.float32) + jnp.dot(active, w_update, preferred_element_type=jnp.float32)
    inv_rms = lax.rsqrt(lax.optimization_barrier(jnp.mean(residual * residual, axis=-1, keepdims=True)) + 1e-06)
    return (residual * inv_rms * gain).astype(jnp.bfloat16)

def pad_global(values):
    values = jnp.pad(values, ((1, 1), (1, 1), (0, 0), (0, 0)), mode='wrap')
    return jnp.pad(values, ((0, 0), (0, 0), (M, M), (0, 0)))

def cheap_layer(state, neighbour_code, radial_basis, w_message, w_update, gain):
    flat_rows = pad_global(state).reshape(-1, state.shape[-1])
    span_y = NY + 2
    span_z = ZM + 2 * M
    coord_z = jnp.arange(ZM, dtype=jnp.int32)[:, None]

    def one_line(line):
        coord_x = line // NY
        coord_y = line % NY
        row_index = neighbour_rows(neighbour_code[coord_x, coord_y], coord_x, coord_y, coord_z, span_y, span_z)
        nearby = flat_rows[row_index]
        summed = jnp.einsum('zsk,zsf->zkf', radial_basis[coord_x, coord_y].astype(jnp.float32), nearby.astype(jnp.float32))
        summed = summed.reshape(ZM, -1).astype(jnp.bfloat16)
        return update(state[coord_x, coord_y], summed, w_message, w_update, gain)
    lines = lax.map(one_line, jnp.arange(NX * NY, dtype=jnp.int32))
    return lines.reshape(state.shape)

def reference(features, neighbour_code, distance, w_message, w_update, norm_gain, w_env, w_out, w_first, w_head, flag_ids, flag_owner, flag_count):
    radial_basis, cutoff = radial(distance)
    state = features
    for layer_index in range(L):
        state = cheap_layer(state, neighbour_code, radial_basis, w_message[layer_index], w_update[layer_index], norm_gain[layer_index])
    flat_state = state.reshape(-1, F)
    projected = jnp.dot(flat_state, w_env, preferred_element_type=jnp.float32).astype(jnp.bfloat16)
    flat_proj = pad_global(projected.reshape(NX, NY, ZM, E)).reshape(-1, E)
    base_force = jnp.einsum('af,cf->ca', flat_state.astype(jnp.float32), w_out.astype(jnp.float32)).reshape(3, NX, NY, ZM)
    span_y = NY + 2
    span_z = ZM + 2 * M
    depth = CZ * M

    def one_device(device):
        index_x = device // (N_GY * N_GZ)
        index_y = device // N_GZ % N_GY
        index_z = device % N_GZ
        local_ids = flag_ids[index_x, index_y, index_z]
        owner = flag_owner[index_x, index_y, index_z, :, 0]
        count = flag_count[index_x, index_y, index_z]
        pos_x = (index_x * CX + local_ids // (CY * depth)).astype(jnp.int32)
        pos_y = (index_y * CY + local_ids // depth % CY).astype(jnp.int32)
        pos_z = (index_z * depth + local_ids % depth).astype(jnp.int32)
        codes = neighbour_code[pos_x, pos_y, pos_z]
        row_index = neighbour_rows(codes, pos_x[:, None], pos_y[:, None], pos_z[:, None], span_y, span_z)
        nearby = flat_proj[row_index]
        environ = (cutoff[pos_x, pos_y, pos_z][..., None] * nearby.astype(jnp.float32)).astype(jnp.bfloat16)
        hidden = jax.nn.silu(jnp.einsum('rse,reh->rsh', environ.astype(jnp.float32), w_first[owner].astype(jnp.float32))).astype(jnp.bfloat16)
        pooled = (lax.optimization_barrier(jnp.sum(hidden.astype(jnp.float32), axis=1)) / K).astype(jnp.bfloat16)
        force = jnp.einsum('rh,rch->rc', pooled.astype(jnp.float32), w_head[owner].astype(jnp.float32))
        alive = (jnp.arange(FLAG_DEV, dtype=jnp.int32) < count).astype(force.dtype)
        return (force * alive[:, None], pos_x, pos_y, pos_z)
    correction, pos_x, pos_y, pos_z = lax.map(one_device, jnp.arange(N_GX * N_GY * N_GZ, dtype=jnp.int32))
    correction = correction.reshape(-1, 3)
    return base_force.at[:, pos_x.reshape(-1), pos_y.reshape(-1), pos_z.reshape(-1)].add(correction.T)
```

```python
import functools

import jax
import jax.numpy as jnp
from jax import lax
from jax.experimental import pallas as pl
from jax.experimental.pallas import tpu as pltpu
from jax.sharding import PartitionSpec as P

M = 4
NRB = 8
L = 2
ROWS = 256
F32 = jnp.float32
BF16 = jnp.bfloat16
MESH = pl.DeviceIdType.MESH


def iota(shape, dim):
    return lax.broadcasted_iota(jnp.int32, shape, dim)


def plane_buffers(n_gx):
    return (1, 0, 1) if n_gx == 2 else (1, 0, 2)


def messages(n_gx):
    steps_x = (0, 1) if n_gx == 2 else (0, 1, -1)
    return [
        (dx, dy, dz)
        for dx in steps_x
        for dy in (0, 1, -1)
        for dz in (0, 1, -1)
        if (dx, dy, dz) != (0, 0, 0)
    ]


def cutoff_of(distance):
    half = distance * (jnp.pi / 10.0)
    sq = half * half
    term = -1.0 / 87178291200.0
    for coef in (1 / 479001600.0, -1 / 3628800.0, 1 / 40320.0, -1 / 720.0, 1 / 24.0, -0.5, 1.0):
        term = term * sq + coef
    return term * term


def face_selector():
    row = iota((96, 128), 0)
    atom = iota((96, 128), 1)
    part = row >> 4
    y = (row & 15) >> 2
    j = row & 3
    g = part - 2
    corner_y = jnp.where((g & 1) == 0, 3, 0)
    corner_z = jnp.where(g < 2, 28, 0)
    corner = jnp.where(y == g, corner_y * 32 + corner_z + j, -1)
    target = jnp.where(part == 0, y * 32 + j, jnp.where(part == 1, y * 32 + 28 + j, corner))
    return jnp.where(atom == target, 1.0, 0.0).astype(BF16)


def candidate_offsets():
    row = iota((ROWS, 128), 0)
    atom = iota((ROWS, 128), 1)
    own_y = atom >> 5
    own_z = (atom & 31) >> 2
    tail = row - 192
    group = (row & 15) >> 2
    col_tail = jnp.where(tail < 32, group + 1, jnp.where((group & 1) == 0, 0, 5))
    col_tail = jnp.where(tail < 48, col_tail, -20)
    z_tail = jnp.where(tail < 16, -1, jnp.where(tail < 32, 8, jnp.where(group < 2, -1, 8)))
    col = jnp.where(row < 192, row >> 5, col_tail)
    z = jnp.where(row < 192, (row & 31) >> 2, z_tail)
    oy = col - own_y
    oz = z - own_z + 1
    good = (oy >= 0) & (oy <= 2) & (oz >= 0) & (oz <= 2)
    return jnp.where(good, oy * 3 + oz, -1)


def potential_kernel(
    sizes,
    feat,
    code,
    dist,
    wm_hbm,
    w_update,
    gain,
    w_env,
    w_out,
    planes_out,
    base_out,
    weights,
    slots,
    dcode,
    offsets,
    near,
    near_proj,
    corner,
    corner_proj,
    packs,
    packs_proj,
    state_ref,
    proj_ref,
    wm,
    send_sem,
    recv_sem,
    wm_sem,
):
    n_gx, n_gy, n_gz = sizes
    buffer_of = plane_buffers(n_gx)
    n_buf = max(buffer_of) + 1
    todo = messages(n_gx)
    me = (lax.axis_index("gx"), lax.axis_index("gy"), lax.axis_index("gz"))

    def target(step):
        return (
            lax.rem(me[0] + step[0] + n_gx, n_gx),
            lax.rem(me[1] + step[1] + n_gy, n_gy),
            me[2] + step[2],
        )

    def along_z(dz, act):
        if dz == 0:
            act()
        elif dz > 0:
            pl.when(me[2] < n_gz - 1)(act)
        else:
            pl.when(me[2] > 0)(act)

    for b in range(n_buf):
        for e in range(2):
            near[e, b, 192:256, :] = jnp.zeros((64, near.shape[-1]), BF16)
        near_proj[b, 192:256, :] = jnp.zeros((64, near_proj.shape[-1]), BF16)
    corner[...] = jnp.zeros(corner.shape, BF16)
    corner_proj[...] = jnp.zeros(corner_proj.shape, BF16)

    barrier = pltpu.get_barrier_semaphore()
    for step in todo:

        def greet(step=step):
            pl.semaphore_signal(barrier, inc=1, device_id=target(step), device_id_type=MESH)

        along_z(step[2], greet)

    weight_copy = pltpu.make_async_copy(wm_hbm, wm, wm_sem)
    weight_copy.start()

    selector = face_selector()

    def copies(e, source, packed, plane, corners):
        made = []
        for index, (dx, dy, dz) in enumerate(todo):
            b = 0 if dx == 0 else buffer_of[0 if dx > 0 else 2]
            if dz == 0:
                if dy == 0:
                    src, dst = source, plane.at[b, pl.ds(32, 128)]
                elif dy > 0:
                    src, dst = source.at[pl.ds(96, 32)], plane.at[b, pl.ds(0, 32)]
                else:
                    src, dst = source.at[pl.ds(0, 32)], plane.at[b, pl.ds(160, 32)]
            elif dy == 0:
                src = packed.at[pl.ds(16 if dz > 0 else 0, 16)]
                dst = plane.at[b, pl.ds(192 if dz > 0 else 208, 16)]
            else:
                g = (0 if dz > 0 else 2) + (0 if dy > 0 else 1)
                src, dst = packed.at[pl.ds(32 + 16 * g, 16)], corners.at[b, g]
            made.append(
                pltpu.make_async_remote_copy(
                    src_ref=src,
                    dst_ref=dst,
                    send_sem=send_sem.at[e, index],
                    recv_sem=recv_sem.at[e, index],
                    device_id=target((dx, dy, dz)),
                    device_id_type=MESH,
                )
            )
        return made

    def send_all(made):
        for step, copy in zip(todo, made):
            along_z(step[2], copy.start)

    def receive_all(made, plane, corners):
        for step, copy in zip(todo, made):
            along_z(-step[2], copy.wait_recv)
        for b in range(n_buf):
            tile = corners[b, 0].astype(F32)
            for g in range(1, 4):
                tile = tile + corners[b, g].astype(F32)
            plane[b, 224:240, :] = tile.astype(BF16)

    def sent_all(made):
        for step, copy in zip(todo, made):
            along_z(step[2], copy.wait_send)

    def pack(state):
        return jnp.dot(selector, state, preferred_element_type=F32).astype(BF16)

    state = feat[0].reshape(128, feat.shape[-1])
    state_ref[0] = state
    packs[0] = pack(state)
    near[0, 0, 32:160, :] = state

    both = (n_buf) * 3
    here = both - 1
    up = jnp.where(me[2] < n_gz - 1, both, 0)
    down = jnp.where(me[2] > 0, both, 0)
    pl.semaphore_wait(barrier, here + up + down)

    first = copies(0, state_ref.at[0], packs.at[0], near.at[0], corner.at[0])
    send_all(first)

    slot_count = code.shape[-1]
    both_rows = jnp.concatenate(
        [dist[0].reshape(128, slot_count), code[0].reshape(128, slot_count).astype(F32)], axis=1
    )
    slots[...] = both_rows.T
    offsets[...] = candidate_offsets()
    for ox in range(3):
        row = iota((72, 128), 0)
        wanted = (((row >> 3) + 9 * ox) * 4 + (row & 3)).astype(F32)

        def put(s, held):
            named = slots[pl.ds(slot_count + s, 1), :]
            return jnp.where(named == wanted, slots[pl.ds(s, 1), :], held)

        dcode[pl.ds(72 * ox, 72), :] = lax.fori_loop(
            0, slot_count, put, jnp.full((72, 128), -1.0, F32), unroll=8
        )

    for b in range(n_buf):
        for half in range(2):
            where_from = offsets[128 * half : 128 * (half + 1), :]
            parts = []
            for ox in range(3):
                if buffer_of[ox] != b:
                    continue
                dense = jnp.full((128, 128), -1.0, F32)
                for p in range(9):
                    rows = dcode[pl.ds((ox * 9 + p) * 8, 8), :]
                    rows = jnp.broadcast_to(rows[None], (16, 8, 128)).reshape(128, 128)
                    dense = jnp.where(where_from == p, rows, dense)
                dense = dense.T
                parts.append((dense, jnp.where(dense > 0.0, cutoff_of(dense), 0.0)))
            for k in range(NRB):
                total = None
                for dense, cut in parts:
                    gap = dense - (0.8 + k * (4.0 / (NRB - 1)))
                    basis = jnp.exp(-2.0 * (gap * gap)) * cut
                    total = basis if total is None else total + basis
                weights[128 * k : 128 * (k + 1), 256 * b + 128 * half : 256 * b + 128 * (half + 1)] = (
                    total.astype(BF16)
                )

    def layer(l, state):
        width = state.shape[-1]
        rows = near[l].reshape(n_buf * ROWS, width)
        message = jnp.zeros((128, width), F32)
        for k in range(NRB):
            summed = jnp.dot(weights[128 * k : 128 * (k + 1), :], rows, preferred_element_type=F32)
            message = message + jnp.dot(
                summed.astype(BF16),
                wm[l, width * k : width * (k + 1), :],
                preferred_element_type=F32,
            )
        active = (message / (1.0 + jnp.exp(-message))).astype(BF16)
        residual = state.astype(F32) + jnp.dot(active, w_update[l], preferred_element_type=F32)
        inv_rms = lax.rsqrt(jnp.mean(residual * residual, axis=-1, keepdims=True) + 1e-06)
        return (residual * inv_rms * gain[l : l + 1, :]).astype(BF16)

    weight_copy.wait()
    receive_all(first, near.at[0], corner.at[0])
    state = layer(0, state)
    state_ref[1] = state
    packs[1] = pack(state)
    second = copies(1, state_ref.at[1], packs.at[1], near.at[1], corner.at[1])
    send_all(second)
    near[1, 0, 32:160, :] = state
    receive_all(second, near.at[1], corner.at[1])
    state = layer(1, state)
    projected = jnp.dot(state, w_env[...], preferred_element_type=F32).astype(BF16)
    proj_ref[...] = projected
    packs_proj[...] = pack(projected)
    third = copies(2, proj_ref, packs_proj, near_proj, corner_proj)
    send_all(third)
    near_proj[0, 32:160, :] = projected
    base_out[...] = lax.dot_general(
        w_out[...], state, (((1,), (1,)), ((), ())), preferred_element_type=F32
    )
    receive_all(third, near_proj, corner_proj)
    planes_out[...] = near_proj[...].reshape(planes_out.shape)
    sent_all(first)
    sent_all(second)
    sent_all(third)


def specialist_kernel(
    n_gx,
    flag_ids,
    owner,
    flag_count,
    code,
    dist,
    planes,
    base,
    w_first,
    w_head,
    out,
    rows_ref,
    cand_ref,
    picked,
    environ,
):
    buffer_of = plane_buffers(n_gx)
    flags = flag_ids.shape[0]
    slot_count = code.shape[-1]
    codes = code[0].reshape(128, slot_count)
    atom = iota((128, slot_count), 0)
    o = lax.div(codes, M)
    j = codes & 3
    ox = lax.div(o, 9)
    oy = lax.rem(lax.div(o, 3), 3)
    oz = lax.rem(o, 3)
    col = (atom >> 5) + oy
    z = ((atom & 31) >> 2) + oz - 1
    inside = (z >= 0) & (z <= 7)
    top = jnp.where(z > 7, 1, 0)
    side = (col == 0) | (col == 5)
    face = 192 + top * 16 + (col - 1) * 4
    edge = 224 + (top * 2 + jnp.where(col == 5, 1, 0)) * 4
    row = jnp.where(inside, col * 32 + z * 4, jnp.where(side, edge, face)) + j
    plane = jnp.where(ox == 1, 0, jnp.where(ox == 0, buffer_of[0], buffer_of[2]))
    cand_ref[...] = (plane * ROWS + row).astype(F32)
    rows_ref[...] = dist[0].reshape(128, slot_count)
    picked[...] = jnp.zeros((128, 128), F32)

    def pick(r, carry):
        q = flag_ids[r]
        picked[pl.ds(r, 1), 0:slot_count] = rows_ref[pl.ds(q, 1), :]
        picked[pl.ds(r, 1), slot_count : 2 * slot_count] = cand_ref[pl.ds(q, 1), :]
        return carry

    lax.fori_loop(0, flags, pick, 0, unroll=8)
    turned = picked[...].T
    cut = cutoff_of(turned[0:slot_count])
    cand = turned[slot_count : 2 * slot_count]
    lanes = iota((slot_count, planes.shape[0]), 1).astype(F32)
    for r in range(flags):
        chosen = jnp.where(cand[:, r : r + 1] == lanes, 1.0, 0.0).astype(BF16)
        nearby = jnp.dot(chosen, planes[...], preferred_element_type=F32)
        environ[slot_count * r : slot_count * (r + 1), :] = (cut[:, r : r + 1] * nearby).astype(BF16)

    lane = iota(base.shape, 1)

    def correct(r, forces):
        p = owner[r]
        rows = environ[pl.ds(pl.multiple_of(r * slot_count, slot_count), slot_count), :]
        wide = jnp.dot(rows, w_first[p], preferred_element_type=F32)
        hidden = (wide / (1.0 + jnp.exp(-wide))).astype(BF16).astype(F32)
        pooled = (jnp.sum(hidden, axis=0, keepdims=True) * (1.0 / slot_count)).astype(BF16)
        terms = pooled.astype(F32) * w_head[p].astype(F32)
        force = jnp.sum(terms, axis=1, keepdims=True)
        live = jnp.where(r < flag_count[0], 1.0, 0.0)
        return forces + jnp.where(lane == flag_ids[r], force * live, 0.0)

    forces = lax.fori_loop(0, flags, correct, base[...], unroll=4)
    for y in range(out.shape[2]):
        out[:, 0, y, :] = forces[:, 32 * y : 32 * (y + 1)]


def per_device(
    features,
    neighbour_code,
    distance,
    w_message,
    w_update,
    norm_gain,
    w_env,
    w_out,
    w_first,
    w_head,
    flag_ids,
    flag_owner,
    flag_count,
):
    sizes = tuple(lax.axis_size(name) for name in ("gx", "gy", "gz"))
    n_buf = max(plane_buffers(sizes[0])) + 1
    feature_width = features.shape[-1]
    env_width = w_env.shape[-1]
    message_count = len(messages(sizes[0]))
    all_first = lax.all_gather(w_first[0], ("gx", "gy"), axis=0)
    all_head = lax.all_gather(w_head[0], ("gx", "gy"), axis=0)

    vmem = pl.BlockSpec(memory_space=pltpu.VMEM)
    smem = pl.BlockSpec(memory_space=pltpu.SMEM)
    planes, base = pl.pallas_call(
        functools.partial(potential_kernel, sizes),
        out_shape=(
            jax.ShapeDtypeStruct((n_buf * ROWS, env_width), BF16),
            jax.ShapeDtypeStruct((3, 128), F32),
        ),
        in_specs=[vmem, vmem, vmem, pl.BlockSpec(memory_space=pl.ANY)] + [vmem] * 4,
        out_specs=(vmem, vmem),
        scratch_shapes=[
            pltpu.VMEM((NRB * 128, n_buf * ROWS), BF16),
            pltpu.VMEM((128, 128), F32),
            pltpu.VMEM((216, 128), F32),
            pltpu.VMEM((ROWS, 128), jnp.int32),
            pltpu.VMEM((2, n_buf, ROWS, feature_width), BF16),
            pltpu.VMEM((n_buf, ROWS, env_width), BF16),
            pltpu.VMEM((2, n_buf, 4, 16, feature_width), BF16),
            pltpu.VMEM((n_buf, 4, 16, env_width), BF16),
            pltpu.VMEM((2, 96, feature_width), BF16),
            pltpu.VMEM((96, env_width), BF16),
            pltpu.VMEM((2, 128, feature_width), BF16),
            pltpu.VMEM((128, env_width), BF16),
            pltpu.VMEM(w_message.shape, BF16),
            pltpu.SemaphoreType.DMA((3, message_count)),
            pltpu.SemaphoreType.DMA((3, message_count)),
            pltpu.SemaphoreType.DMA,
        ],
        compiler_params=pltpu.CompilerParams(
            collective_id=0, has_side_effects=True, vmem_limit_bytes=32 * 1024 * 1024
        ),
        cost_estimate=pl.CostEstimate(flops=10**9, bytes_accessed=4 * 10**6, transcendentals=10**6),
        name="potential",
    )(features, neighbour_code, distance, w_message, w_update, norm_gain, w_env, w_out)

    owner = flag_owner.reshape(-1)
    if all_first.shape[0] > 8:
        all_first = all_first[owner]
        all_head = all_head[owner]
        owner = jnp.arange(owner.shape[0], dtype=jnp.int32)
    local_ids = flag_ids.reshape(-1)
    flags = local_ids.shape[0]
    slot_count = distance.shape[-1]
    return pl.pallas_call(
        functools.partial(specialist_kernel, sizes[0]),
        out_shape=jax.ShapeDtypeStruct((3,) + features.shape[:3], F32),
        in_specs=[smem] * 3 + [vmem] * 6,
        out_specs=vmem,
        scratch_shapes=[
            pltpu.VMEM((128, slot_count), F32),
            pltpu.VMEM((128, slot_count), F32),
            pltpu.VMEM((128, 128), F32),
            pltpu.VMEM((flags * slot_count, env_width), BF16),
        ],
        compiler_params=pltpu.CompilerParams(vmem_limit_bytes=40 * 1024 * 1024),
        cost_estimate=pl.CostEstimate(
            flops=10**9, bytes_accessed=3 * 10**6, transcendentals=2 * 10**6
        ),
        name="specialist",
    )(
        local_ids,
        owner,
        flag_count.reshape(-1),
        neighbour_code,
        distance,
        planes,
        base,
        all_first,
        all_head,
    )


def solution(mesh):
    placed = (
        P("gx", "gy", "gz", None),
        P("gx", "gy", "gz", None),
        P("gx", "gy", "gz", None),
        P(),
        P(),
        P(),
        P(),
        P(),
        P(("gx", "gy"), None, None),
        P(("gx", "gy"), None, None),
        P("gx", "gy", "gz", None),
        P("gx", "gy", "gz", None, None),
        P("gx", "gy", "gz"),
    )
    return jax.shard_map(
        per_device, mesh=mesh, in_specs=placed, out_specs=P(None, "gx", "gy", "gz"), check_vma=False
    )
```

```python
import functools

import jax
import jax.numpy as jnp
from jax import lax
from jax.experimental import pallas as pl
from jax.experimental.pallas import tpu as pltpu
from jax.sharding import PartitionSpec as P

M = 4
NRB = 8
L = 2
ROWS = 256
F32 = jnp.float32
BF16 = jnp.bfloat16
MESH = pl.DeviceIdType.MESH


def iota(shape, dim):
    return lax.broadcasted_iota(jnp.int32, shape, dim)


def plane_buffers(n_gx):
    return (1, 0, 1) if n_gx == 2 else (1, 0, 2)


def messages(n_gx):
    steps_x = (0, 1) if n_gx == 2 else (0, 1, -1)
    return [
        (dx, dy, dz)
        for dx in steps_x
        for dy in (0, 1, -1)
        for dz in (0, 1, -1)
        if (dx, dy, dz) != (0, 0, 0)
    ]


def cutoff_of(distance):
    half = distance * (jnp.pi / 10.0)
    sq = half * half
    term = -1.0 / 87178291200.0
    for coef in (1 / 479001600.0, -1 / 3628800.0, 1 / 40320.0, -1 / 720.0, 1 / 24.0, -0.5, 1.0):
        term = term * sq + coef
    return term * term


def face_selector():
    row = iota((96, 128), 0)
    atom = iota((96, 128), 1)
    part = row >> 4
    y = (row & 15) >> 2
    j = row & 3
    g = part - 2
    corner_y = jnp.where((g & 1) == 0, 3, 0)
    corner_z = jnp.where(g < 2, 28, 0)
    corner = jnp.where(y == g, corner_y * 32 + corner_z + j, -1)
    target = jnp.where(part == 0, y * 32 + j, jnp.where(part == 1, y * 32 + 28 + j, corner))
    return jnp.where(atom == target, 1.0, 0.0).astype(BF16)


def candidate_offsets():
    row = iota((ROWS, 128), 0)
    atom = iota((ROWS, 128), 1)
    own_y = atom >> 5
    own_z = (atom & 31) >> 2
    tail = row - 192
    group = (row & 15) >> 2
    col_tail = jnp.where(tail < 32, group + 1, jnp.where((group & 1) == 0, 0, 5))
    col_tail = jnp.where(tail < 48, col_tail, -20)
    z_tail = jnp.where(tail < 16, -1, jnp.where(tail < 32, 8, jnp.where(group < 2, -1, 8)))
    col = jnp.where(row < 192, row >> 5, col_tail)
    z = jnp.where(row < 192, (row & 31) >> 2, z_tail)
    oy = col - own_y
    oz = z - own_z + 1
    good = (oy >= 0) & (oy <= 2) & (oz >= 0) & (oz <= 2)
    return jnp.where(good, oy * 3 + oz, -1)


def force_kernel(
    sizes,
    inside,
    flag_ids,
    owner,
    flag_count,
    feat_hbm,
    code_hbm,
    dist_hbm,
    wm_hbm,
    wu_hbm,
    w_env_hbm,
    first_hbm,
    gain,
    w_out,
    head,
    out,
    feat,
    code,
    dist,
    wm,
    w_update,
    w_env,
    models,
    weights,
    slots,
    dcode,
    offsets,
    near,
    near_proj,
    corner,
    corner_proj,
    packs,
    packs_proj,
    state_ref,
    proj_ref,
    cand_ref,
    dense_rows,
    picked,
    environ,
    send_sem,
    recv_sem,
    model_send,
    model_recv,
    load_sem,
):
    n_gx, n_gy, n_gz = sizes
    buffer_of = plane_buffers(n_gx)
    n_buf = max(buffer_of) + 1
    todo = messages(n_gx)
    me = (lax.axis_index("gx"), lax.axis_index("gy"), lax.axis_index("gz"))

    def target(step):
        return (
            lax.rem(me[0] + step[0] + n_gx, n_gx),
            lax.rem(me[1] + step[1] + n_gy, n_gy),
            me[2] + step[2],
        )

    def along_z(dz, act):
        if dz == 0:
            act()
        elif dz > 0:
            pl.when(me[2] < n_gz - 1)(act)
        else:
            pl.when(me[2] > 0)(act)

    def load(index, source, held):
        copy = pltpu.make_async_copy(source, held, load_sem.at[index])
        copy.start()
        return copy

    loads = [
        load(index, source, held)
        for index, (source, held) in enumerate(
            ((feat_hbm, feat), (code_hbm, code), (dist_hbm, dist))
        )
    ]
    mine = me[0] * n_gy + me[1]
    if inside:
        first_load = load(3, first_hbm.at[0], models.at[mine, pl.ds(0, 128)])
    else:
        first_load = load(3, first_hbm, models)
    late_loads = [
        load(4 + index, source, held)
        for index, (source, held) in enumerate(
            ((wm_hbm, wm), (wu_hbm, w_update), (w_env_hbm, w_env))
        )
    ]
    if inside:
        models[pl.ds(mine, 1), 128:144, :] = jnp.zeros((1, 16, models.shape[-1]), BF16)
        models[pl.ds(mine, 1), 128:131, :] = head[...]

    for b in range(n_buf):
        for e in range(2):
            near[e, b, 192:256, :] = jnp.zeros((64, near.shape[-1]), BF16)
        near_proj[b, 192:256, :] = jnp.zeros((64, near_proj.shape[-1]), BF16)
    corner[...] = jnp.zeros(corner.shape, BF16)
    corner_proj[...] = jnp.zeros(corner_proj.shape, BF16)

    barrier = pltpu.get_barrier_semaphore()
    for step in todo:

        def greet(step=step):
            pl.semaphore_signal(barrier, inc=1, device_id=target(step), device_id_type=MESH)

        along_z(step[2], greet)

    if inside:
        for dx in range(2):
            pl.semaphore_signal(
                barrier, inc=1, device_id=target((dx, 2, 0)), device_id_type=MESH
            )

    selector = face_selector()

    def copies(e, source, packed, plane, corners):
        made = []
        for index, (dx, dy, dz) in enumerate(todo):
            b = 0 if dx == 0 else buffer_of[0 if dx > 0 else 2]
            if dz == 0:
                if dy == 0:
                    src, dst = source, plane.at[b, pl.ds(32, 128)]
                elif dy > 0:
                    src, dst = source.at[pl.ds(96, 32)], plane.at[b, pl.ds(0, 32)]
                else:
                    src, dst = source.at[pl.ds(0, 32)], plane.at[b, pl.ds(160, 32)]
            elif dy == 0:
                src = packed.at[pl.ds(16 if dz > 0 else 0, 16)]
                dst = plane.at[b, pl.ds(192 if dz > 0 else 208, 16)]
            else:
                g = (0 if dz > 0 else 2) + (0 if dy > 0 else 1)
                src, dst = packed.at[pl.ds(32 + 16 * g, 16)], corners.at[b, g]
            made.append(
                pltpu.make_async_remote_copy(
                    src_ref=src,
                    dst_ref=dst,
                    send_sem=send_sem.at[e, index],
                    recv_sem=recv_sem.at[e, index],
                    device_id=target((dx, dy, dz)),
                    device_id_type=MESH,
                )
            )
        return made

    def send_all(made):
        for step, copy in zip(todo, made):
            along_z(step[2], copy.start)

    def receive_all(made, plane, corners):
        for step, copy in zip(todo, made):
            along_z(-step[2], copy.wait_recv)
        for b in range(n_buf):
            tile = corners[b, 0].astype(F32)
            for g in range(1, 4):
                tile = tile + corners[b, g].astype(F32)
            plane[b, 224:240, :] = tile.astype(BF16)

    def sent_all(made):
        for step, copy in zip(todo, made):
            along_z(step[2], copy.wait_send)

    shift_y, shift_x, sibling = (
        (lax.rem(me[0] + 1, n_gx), me[1]),
        (me[0], lax.rem(me[1] + 2, n_gy)),
        (me[0], me[1] + 1 - 2 * lax.rem(me[1], 2)),
    )

    def model_copy(index, shard, rows, to):
        part = models.at[shard[0] * n_gy + shard[1], pl.ds(*rows)]
        return pltpu.make_async_remote_copy(
            src_ref=part,
            dst_ref=part,
            send_sem=model_send.at[index],
            recv_sem=model_recv.at[index],
            device_id=(to[0], to[1], me[2]),
            device_id_type=MESH,
        )

    whole_shard = (0, 144)
    model_copies = [
        model_copy(0, me, whole_shard, shift_y),
        model_copy(1, me, whole_shard, shift_x),
        model_copy(2, me, whole_shard, sibling),
        model_copy(3, shift_x, (0, 64), shift_y),
        model_copy(4, shift_y, (64, 80), shift_x),
        model_copy(5, shift_y, whole_shard, sibling),
        model_copy(6, shift_x, whole_shard, sibling),
        model_copy(7, (shift_y[0], shift_x[1]), whole_shard, sibling),
    ] if inside else []

    def pack(state):
        return jnp.dot(selector, state, preferred_element_type=F32).astype(BF16)

    loads[0].wait()
    state = feat[0].reshape(128, feat.shape[-1])
    state_ref[0] = state
    packs[0] = pack(state)
    near[0, 0, 32:160, :] = state

    both = (n_buf) * 3
    here = both - 1 + (2 if inside else 0)
    up = jnp.where(me[2] < n_gz - 1, both, 0)
    down = jnp.where(me[2] > 0, both, 0)
    pl.semaphore_wait(barrier, here + up + down)

    first = copies(0, state_ref.at[0], packs.at[0], near.at[0], corner.at[0])
    send_all(first)
    first_load.wait()
    for copy in model_copies[:3]:
        copy.start()

    loads[1].wait()
    loads[2].wait()
    slot_count = code.shape[-1]
    both_rows = jnp.concatenate(
        [dist[0].reshape(128, slot_count), code[0].reshape(128, slot_count).astype(F32)], axis=1
    )
    slots[...] = both_rows.T
    offsets[...] = candidate_offsets()
    for ox in range(3):
        row = iota((72, 128), 0)
        wanted = (((row >> 3) + 9 * ox) * 4 + (row & 3)).astype(F32)

        def put(s, held):
            named = slots[pl.ds(slot_count + s, 1), :]
            return jnp.where(named == wanted, slots[pl.ds(s, 1), :], held)

        dcode[pl.ds(72 * ox, 72), :] = lax.fori_loop(
            0, slot_count, put, jnp.full((72, 128), -1.0, F32), unroll=8
        )

    for b in range(n_buf):
        for half in range(2):
            where_from = offsets[128 * half : 128 * (half + 1), :]
            parts = []
            for ox in range(3):
                if buffer_of[ox] != b:
                    continue
                dense = jnp.full((128, 128), -1.0, F32)
                for p in range(9):
                    rows = dcode[pl.ds((ox * 9 + p) * 8, 8), :]
                    rows = jnp.broadcast_to(rows[None], (16, 8, 128)).reshape(128, 128)
                    dense = jnp.where(where_from == p, rows, dense)
                dense = dense.T
                parts.append((dense, jnp.where(dense > 0.0, cutoff_of(dense), 0.0)))
            for k in range(NRB):
                total = None
                for dense, cut in parts:
                    gap = dense - (0.8 + k * (4.0 / (NRB - 1)))
                    basis = jnp.exp(-2.0 * (gap * gap)) * cut
                    total = basis if total is None else total + basis
                weights[128 * k : 128 * (k + 1), 256 * b + 128 * half : 256 * b + 128 * (half + 1)] = (
                    total.astype(BF16)
                )

    def layer(l, state):
        width = state.shape[-1]
        rows = near[l].reshape(n_buf * ROWS, width)
        message = jnp.zeros((128, width), F32)
        for k in range(NRB):
            summed = jnp.dot(weights[128 * k : 128 * (k + 1), :], rows, preferred_element_type=F32)
            message = message + jnp.dot(
                summed.astype(BF16),
                wm[l, width * k : width * (k + 1), :],
                preferred_element_type=F32,
            )
        active = (message / (1.0 + jnp.exp(-message))).astype(BF16)
        residual = state.astype(F32) + jnp.dot(active, w_update[l], preferred_element_type=F32)
        inv_rms = lax.rsqrt(jnp.mean(residual * residual, axis=-1, keepdims=True) + 1e-06)
        return (residual * inv_rms * gain[l : l + 1, :]).astype(BF16)

    for copy in late_loads:
        copy.wait()
    receive_all(first, near.at[0], corner.at[0])
    state = layer(0, state)
    state_ref[1] = state
    packs[1] = pack(state)
    second = copies(1, state_ref.at[1], packs.at[1], near.at[1], corner.at[1])
    send_all(second)
    if inside:
        model_copies[0].wait_recv()
        model_copies[1].wait_recv()
        for copy in model_copies[3:7]:
            copy.start()
    near[1, 0, 32:160, :] = state
    receive_all(second, near.at[1], corner.at[1])
    state = layer(1, state)
    projected = jnp.dot(state, w_env[...], preferred_element_type=F32).astype(BF16)
    proj_ref[...] = projected
    packs_proj[...] = pack(projected)
    third = copies(2, proj_ref, packs_proj, near_proj, corner_proj)
    send_all(third)
    near_proj[0, 32:160, :] = projected
    if inside:
        model_copies[3].wait_recv()
        model_copies[4].wait_recv()
        model_copies[7].start()
    base = lax.dot_general(
        w_out[...], state, (((1,), (1,)), ((), ())), preferred_element_type=F32
    )
    flags = flag_ids.shape[0]
    codes = code[0].reshape(128, slot_count)
    atom = iota((128, slot_count), 0)
    o = lax.div(codes, M)
    j = codes & 3
    ox = lax.div(o, 9)
    oy = lax.rem(lax.div(o, 3), 3)
    oz = lax.rem(o, 3)
    col = (atom >> 5) + oy
    z = ((atom & 31) >> 2) + oz - 1
    within = (z >= 0) & (z <= 7)
    top = jnp.where(z > 7, 1, 0)
    side = (col == 0) | (col == 5)
    face = 192 + top * 16 + (col - 1) * 4
    edge = 224 + (top * 2 + jnp.where(col == 5, 1, 0)) * 4
    row = jnp.where(within, col * 32 + z * 4, jnp.where(side, edge, face)) + j
    plane = jnp.where(ox == 1, 0, jnp.where(ox == 0, buffer_of[0], buffer_of[2]))
    cand_ref[...] = (plane * ROWS + row).astype(F32)
    dense_rows[...] = dist[0].reshape(128, slot_count)
    picked[...] = jnp.zeros((128, 128), F32)

    def pick(r, carry):
        q = flag_ids[r]
        picked[pl.ds(r, 1), 0:slot_count] = dense_rows[pl.ds(q, 1), :]
        picked[pl.ds(r, 1), slot_count : 2 * slot_count] = cand_ref[pl.ds(q, 1), :]
        return carry

    lax.fori_loop(0, flags, pick, 0, unroll=8)
    turned = picked[...].T
    cut = cutoff_of(turned[0:slot_count])
    cand = turned[slot_count : 2 * slot_count]
    receive_all(third, near_proj, corner_proj)
    lanes = iota((slot_count, n_buf * ROWS), 1).astype(F32)
    planes = near_proj[...].reshape(n_buf * ROWS, near_proj.shape[-1])
    for r in range(flags):
        chosen = jnp.where(cand[:, r : r + 1] == lanes, 1.0, 0.0).astype(BF16)
        nearby = jnp.dot(chosen, planes, preferred_element_type=F32)
        environ[slot_count * r : slot_count * (r + 1), :] = (cut[:, r : r + 1] * nearby).astype(BF16)

    if inside:
        for copy in (model_copies[2], *model_copies[5:]):
            copy.wait_recv()
    lane = iota(base.shape, 1)

    def correct(r, forces):
        p = owner[r]
        rows = environ[pl.ds(pl.multiple_of(r * slot_count, slot_count), slot_count), :]
        wide = jnp.dot(rows, models[p, 0:128, :], preferred_element_type=F32)
        hidden = (wide / (1.0 + jnp.exp(-wide))).astype(BF16).astype(F32)
        pooled = (jnp.sum(hidden, axis=0, keepdims=True) * (1.0 / slot_count)).astype(BF16)
        terms = pooled.astype(F32) * (models[p, 128:131, :] if inside else head[p]).astype(F32)
        force = jnp.sum(terms, axis=1, keepdims=True)
        live = jnp.where(r < flag_count[0], 1.0, 0.0)
        return forces + jnp.where(lane == flag_ids[r], force * live, 0.0)

    forces = lax.fori_loop(0, flags, correct, base, unroll=4)
    for y in range(out.shape[2]):
        out[:, 0, y, :] = forces[:, 32 * y : 32 * (y + 1)]
    sent_all(first)
    sent_all(second)
    sent_all(third)
    for copy in model_copies:
        copy.wait_send()


def per_device(
    features,
    neighbour_code,
    distance,
    w_message,
    w_update,
    norm_gain,
    w_env,
    w_out,
    w_first,
    w_head,
    flag_ids,
    flag_owner,
    flag_count,
):
    sizes = tuple(lax.axis_size(name) for name in ("gx", "gy", "gz"))
    n_buf = max(plane_buffers(sizes[0])) + 1
    feature_width = features.shape[-1]
    env_width = w_env.shape[-1]
    message_count = len(messages(sizes[0]))
    local_ids = flag_ids.reshape(-1)
    owner = flag_owner.reshape(-1)
    flags = local_ids.shape[0]
    slot_count = distance.shape[-1]
    inside = sizes[:2] == (2, 4)
    if inside:
        models_shape = (8, 144, w_first.shape[-1])
    else:
        w_first = lax.all_gather(w_first[0], ("gx", "gy"), axis=0)[owner]
        w_head = lax.all_gather(w_head[0], ("gx", "gy"), axis=0)[owner]
        owner = jnp.arange(flags, dtype=jnp.int32)
        models_shape = w_first.shape

    vmem = pl.BlockSpec(memory_space=pltpu.VMEM)
    smem = pl.BlockSpec(memory_space=pltpu.SMEM)
    anywhere = pl.BlockSpec(memory_space=pl.ANY)
    return pl.pallas_call(
        functools.partial(force_kernel, sizes, inside),
        out_shape=jax.ShapeDtypeStruct((3,) + features.shape[:3], F32),
        in_specs=[smem] * 3 + [anywhere] * 7 + [vmem] * 3,
        out_specs=vmem,
        scratch_shapes=[
            pltpu.VMEM(features.shape, BF16),
            pltpu.VMEM(neighbour_code.shape, jnp.int32),
            pltpu.VMEM(distance.shape, F32),
            pltpu.VMEM(w_message.shape, BF16),
            pltpu.VMEM(w_update.shape, BF16),
            pltpu.VMEM(w_env.shape, BF16),
            pltpu.VMEM(models_shape, BF16),
            pltpu.VMEM((NRB * 128, n_buf * ROWS), BF16),
            pltpu.VMEM((128, 128), F32),
            pltpu.VMEM((216, 128), F32),
            pltpu.VMEM((ROWS, 128), jnp.int32),
            pltpu.VMEM((2, n_buf, ROWS, feature_width), BF16),
            pltpu.VMEM((n_buf, ROWS, env_width), BF16),
            pltpu.VMEM((2, n_buf, 4, 16, feature_width), BF16),
            pltpu.VMEM((n_buf, 4, 16, env_width), BF16),
            pltpu.VMEM((2, 96, feature_width), BF16),
            pltpu.VMEM((96, env_width), BF16),
            pltpu.VMEM((2, 128, feature_width), BF16),
            pltpu.VMEM((128, env_width), BF16),
            pltpu.VMEM((128, slot_count), F32),
            pltpu.VMEM((128, slot_count), F32),
            pltpu.VMEM((128, 128), F32),
            pltpu.VMEM((flags * slot_count, env_width), BF16),
            pltpu.SemaphoreType.DMA((3, message_count)),
            pltpu.SemaphoreType.DMA((3, message_count)),
            pltpu.SemaphoreType.DMA((8,)),
            pltpu.SemaphoreType.DMA((8,)),
            pltpu.SemaphoreType.DMA((7,)),
        ],
        compiler_params=pltpu.CompilerParams(
            collective_id=0, has_side_effects=True, vmem_limit_bytes=56 * 1024 * 1024
        ),
        cost_estimate=pl.CostEstimate(
            flops=2 * 10**9, bytes_accessed=4 * 10**6, transcendentals=3 * 10**6
        ),
        name="forces",
    )(
        local_ids,
        owner,
        flag_count.reshape(-1),
        features,
        neighbour_code,
        distance,
        w_message,
        w_update,
        w_env,
        w_first,
        norm_gain,
        w_out,
        w_head,
    )


def solution(mesh):
    placed = (
        P("gx", "gy", "gz", None),
        P("gx", "gy", "gz", None),
        P("gx", "gy", "gz", None),
        P(),
        P(),
        P(),
        P(),
        P(),
        P(("gx", "gy"), None, None),
        P(("gx", "gy"), None, None),
        P("gx", "gy", "gz", None),
        P("gx", "gy", "gz", None, None),
        P("gx", "gy", "gz"),
    )
    return jax.shard_map(
        per_device, mesh=mesh, in_specs=placed, out_specs=P(None, "gx", "gy", "gz"), check_vma=False
    )
```

```python
import functools

import jax
import jax.numpy as jnp
from jax import lax
from jax.experimental import pallas as pl
from jax.experimental.pallas import tpu as pltpu
from jax.sharding import PartitionSpec as P

M = 4
NRB = 8
L = 2
ROWS = 256
F32 = jnp.float32
BF16 = jnp.bfloat16
MESH = pl.DeviceIdType.MESH


def iota(shape, dim):
    return lax.broadcasted_iota(jnp.int32, shape, dim)


def plane_buffers(n_gx):
    return (1, 0, 1) if n_gx == 2 else (1, 0, 2)


def messages(n_gx):
    steps_x = (0, 1) if n_gx == 2 else (0, 1, -1)
    return [
        (dx, dy, dz)
        for dx in steps_x
        for dy in (0, 1, -1)
        for dz in (0, 1, -1)
        if (dx, dy, dz) != (0, 0, 0)
    ]


def cutoff_of(distance):
    half = distance * (jnp.pi / 10.0)
    sq = half * half
    term = -1.0 / 87178291200.0
    for coef in (1 / 479001600.0, -1 / 3628800.0, 1 / 40320.0, -1 / 720.0, 1 / 24.0, -0.5, 1.0):
        term = term * sq + coef
    return term * term


def face_selector():
    row = iota((96, 128), 0)
    atom = iota((96, 128), 1)
    part = row >> 4
    y = (row & 15) >> 2
    j = row & 3
    g = part - 2
    corner_y = jnp.where((g & 1) == 0, 3, 0)
    corner_z = jnp.where(g < 2, 28, 0)
    corner = jnp.where(y == g, corner_y * 32 + corner_z + j, -1)
    target = jnp.where(part == 0, y * 32 + j, jnp.where(part == 1, y * 32 + 28 + j, corner))
    return jnp.where(atom == target, 1.0, 0.0).astype(BF16)


def candidate_offsets():
    row = iota((ROWS, 128), 0)
    atom = iota((ROWS, 128), 1)
    own_y = atom >> 5
    own_z = (atom & 31) >> 2
    tail = row - 192
    group = (row & 15) >> 2
    col_tail = jnp.where(tail < 32, group + 1, jnp.where((group & 1) == 0, 0, 5))
    col_tail = jnp.where(tail < 48, col_tail, -20)
    z_tail = jnp.where(tail < 16, -1, jnp.where(tail < 32, 8, jnp.where(group < 2, -1, 8)))
    col = jnp.where(row < 192, row >> 5, col_tail)
    z = jnp.where(row < 192, (row & 31) >> 2, z_tail)
    oy = col - own_y
    oz = z - own_z + 1
    good = (oy >= 0) & (oy <= 2) & (oz >= 0) & (oz <= 2)
    return jnp.where(good, oy * 3 + oz, -1)


def force_kernel(
    sizes,
    inside,
    flag_ids,
    owner,
    flag_count,
    feat_hbm,
    code_hbm,
    dist_hbm,
    wm_hbm,
    wu_hbm,
    w_env_hbm,
    first_hbm,
    gain,
    w_out,
    head,
    out,
    feat,
    code,
    dist,
    wm,
    w_update,
    w_env,
    models,
    weights,
    slots,
    dcode,
    offsets,
    near,
    near_proj,
    corner,
    corner_proj,
    packs,
    packs_proj,
    state_ref,
    proj_ref,
    cand_ref,
    dense_rows,
    picked,
    environ,
    chosen,
    send_sem,
    recv_sem,
    model_send,
    model_recv,
    load_sem,
):
    n_gx, n_gy, n_gz = sizes
    buffer_of = plane_buffers(n_gx)
    n_buf = max(buffer_of) + 1
    todo = messages(n_gx)
    me = (lax.axis_index("gx"), lax.axis_index("gy"), lax.axis_index("gz"))

    def target(step):
        return (
            lax.rem(me[0] + step[0] + n_gx, n_gx),
            lax.rem(me[1] + step[1] + n_gy, n_gy),
            me[2] + step[2],
        )

    def along_z(dz, act):
        if dz == 0:
            act()
        elif dz > 0:
            pl.when(me[2] < n_gz - 1)(act)
        else:
            pl.when(me[2] > 0)(act)

    def load(index, source, held):
        copy = pltpu.make_async_copy(source, held, load_sem.at[index])
        copy.start()
        return copy

    loads = [
        load(index, source, held)
        for index, (source, held) in enumerate(
            ((feat_hbm, feat), (code_hbm, code), (dist_hbm, dist))
        )
    ]
    mine = me[0] * n_gy + me[1]
    if inside:
        first_load = load(3, first_hbm.at[0], models.at[mine, pl.ds(0, 128)])
    else:
        first_load = load(3, first_hbm, models)
    late_loads = [
        load(4 + index, source, held)
        for index, (source, held) in enumerate(
            ((wm_hbm, wm), (wu_hbm, w_update), (w_env_hbm, w_env))
        )
    ]
    if inside:
        models[pl.ds(mine, 1), 128:144, :] = jnp.zeros((1, 16, models.shape[-1]), BF16)
        models[pl.ds(mine, 1), 128:131, :] = head[...]

    for b in range(n_buf):
        for e in range(2):
            near[e, b, 192:256, :] = jnp.zeros((64, near.shape[-1]), BF16)
        near_proj[b, 192:256, :] = jnp.zeros((64, near_proj.shape[-1]), BF16)
    corner[...] = jnp.zeros(corner.shape, BF16)
    corner_proj[...] = jnp.zeros(corner_proj.shape, BF16)

    barrier = pltpu.get_barrier_semaphore()
    for step in todo:

        def greet(step=step):
            pl.semaphore_signal(barrier, inc=1, device_id=target(step), device_id_type=MESH)

        along_z(step[2], greet)

    if inside:
        for dx in range(2):
            pl.semaphore_signal(
                barrier, inc=1, device_id=target((dx, 2, 0)), device_id_type=MESH
            )

    selector = face_selector()

    def copies(e, source, packed, plane, corners):
        made = []
        for index, (dx, dy, dz) in enumerate(todo):
            b = 0 if dx == 0 else buffer_of[0 if dx > 0 else 2]
            if dz == 0:
                if dy == 0:
                    src, dst = source, plane.at[b, pl.ds(32, 128)]
                elif dy > 0:
                    src, dst = source.at[pl.ds(96, 32)], plane.at[b, pl.ds(0, 32)]
                else:
                    src, dst = source.at[pl.ds(0, 32)], plane.at[b, pl.ds(160, 32)]
            elif dy == 0:
                src = packed.at[pl.ds(16 if dz > 0 else 0, 16)]
                dst = plane.at[b, pl.ds(192 if dz > 0 else 208, 16)]
            else:
                g = (0 if dz > 0 else 2) + (0 if dy > 0 else 1)
                src, dst = packed.at[pl.ds(32 + 16 * g, 16)], corners.at[b, g]
            made.append(
                pltpu.make_async_remote_copy(
                    src_ref=src,
                    dst_ref=dst,
                    send_sem=send_sem.at[e, index],
                    recv_sem=recv_sem.at[e, index],
                    device_id=target((dx, dy, dz)),
                    device_id_type=MESH,
                )
            )
        return made

    def send_all(made):
        for step, copy in zip(todo, made):
            along_z(step[2], copy.start)

    def receive_all(made, plane, corners):
        for step, copy in zip(todo, made):
            along_z(-step[2], copy.wait_recv)
        for b in range(n_buf):
            tile = corners[b, 0].astype(F32)
            for g in range(1, 4):
                tile = tile + corners[b, g].astype(F32)
            plane[b, 224:240, :] = tile.astype(BF16)

    def sent_all(made):
        for step, copy in zip(todo, made):
            along_z(step[2], copy.wait_send)

    shift_y, shift_x, sibling = (
        (lax.rem(me[0] + 1, n_gx), me[1]),
        (me[0], lax.rem(me[1] + 2, n_gy)),
        (me[0], me[1] + 1 - 2 * lax.rem(me[1], 2)),
    )

    def model_copy(index, shard, rows, to):
        part = models.at[shard[0] * n_gy + shard[1], pl.ds(*rows)]
        return pltpu.make_async_remote_copy(
            src_ref=part,
            dst_ref=part,
            send_sem=model_send.at[index],
            recv_sem=model_recv.at[index],
            device_id=(to[0], to[1], me[2]),
            device_id_type=MESH,
        )

    whole_shard = (0, 144)
    model_copies = [
        model_copy(0, me, whole_shard, shift_y),
        model_copy(1, me, whole_shard, shift_x),
        model_copy(2, me, whole_shard, sibling),
        model_copy(3, shift_x, (0, 64), shift_y),
        model_copy(4, shift_y, (64, 80), shift_x),
        model_copy(5, shift_y, whole_shard, sibling),
        model_copy(6, shift_x, whole_shard, sibling),
        model_copy(7, (shift_y[0], shift_x[1]), whole_shard, sibling),
    ] if inside else []

    def pack(state):
        return jnp.dot(selector, state, preferred_element_type=F32).astype(BF16)

    loads[0].wait()
    state = feat[0].reshape(128, feat.shape[-1])
    state_ref[0] = state
    packs[0] = pack(state)
    near[0, 0, 32:160, :] = state

    both = (n_buf) * 3
    here = both - 1 + (2 if inside else 0)
    up = jnp.where(me[2] < n_gz - 1, both, 0)
    down = jnp.where(me[2] > 0, both, 0)
    pl.semaphore_wait(barrier, here + up + down)

    first = copies(0, state_ref.at[0], packs.at[0], near.at[0], corner.at[0])
    send_all(first)
    first_load.wait()
    for copy in model_copies[:3]:
        copy.start()

    loads[1].wait()
    loads[2].wait()
    slot_count = code.shape[-1]
    both_rows = jnp.concatenate(
        [dist[0].reshape(128, slot_count), code[0].reshape(128, slot_count).astype(F32)], axis=1
    )
    slots[...] = both_rows.T
    offsets[...] = candidate_offsets()
    for ox in range(3):
        row = iota((72, 128), 0)
        wanted = (((row >> 3) + 9 * ox) * 4 + (row & 3)).astype(F32)

        def put(s, held):
            named = slots[pl.ds(slot_count + s, 1), :]
            return jnp.where(named == wanted, slots[pl.ds(s, 1), :], held)

        dcode[pl.ds(72 * ox, 72), :] = lax.fori_loop(
            0, slot_count, put, jnp.full((72, 128), -1.0, F32), unroll=8
        )

    for b in range(n_buf):
        for half in range(2):
            where_from = offsets[128 * half : 128 * (half + 1), :]
            parts = []
            for ox in range(3):
                if buffer_of[ox] != b:
                    continue
                dense = jnp.full((128, 128), -1.0, F32)
                for p in range(9):
                    rows = dcode[pl.ds((ox * 9 + p) * 8, 8), :]
                    rows = jnp.broadcast_to(rows[None], (16, 8, 128)).reshape(128, 128)
                    dense = jnp.where(where_from == p, rows, dense)
                dense = dense.T
                parts.append((dense, jnp.where(dense > 0.0, cutoff_of(dense), 0.0)))
            for k in range(NRB):
                total = None
                for dense, cut in parts:
                    gap = dense - (0.8 + k * (4.0 / (NRB - 1)))
                    basis = jnp.exp(-2.0 * (gap * gap)) * cut
                    total = basis if total is None else total + basis
                weights[128 * k : 128 * (k + 1), 256 * b + 128 * half : 256 * b + 128 * (half + 1)] = (
                    total.astype(BF16)
                )

    def layer(l, state):
        width = state.shape[-1]
        rows = near[l].reshape(n_buf * ROWS, width)
        summed = jnp.dot(weights[...], rows, preferred_element_type=F32).astype(BF16)
        summed = jnp.concatenate([summed[128 * k : 128 * (k + 1)] for k in range(NRB)], axis=1)
        half = 0.5 * jnp.dot(summed, wm[l], preferred_element_type=F32)
        active = (half + half * jnp.tanh(half)).astype(BF16)
        residual = state.astype(F32) + jnp.dot(active, w_update[l], preferred_element_type=F32)
        inv_rms = lax.rsqrt(jnp.mean(residual * residual, axis=-1, keepdims=True) + 1e-06)
        return (residual * inv_rms * gain[l : l + 1, :]).astype(BF16)

    for copy in late_loads:
        copy.wait()
    receive_all(first, near.at[0], corner.at[0])
    state = layer(0, state)
    state_ref[1] = state
    packs[1] = pack(state)
    second = copies(1, state_ref.at[1], packs.at[1], near.at[1], corner.at[1])
    send_all(second)
    near[1, 0, 32:160, :] = state
    flags = flag_ids.shape[0]
    codes = code[0].reshape(128, slot_count)
    atom = iota((128, slot_count), 0)
    o = lax.div(codes, M)
    j = codes & 3
    ox = lax.div(o, 9)
    oy = lax.rem(lax.div(o, 3), 3)
    oz = lax.rem(o, 3)
    col = (atom >> 5) + oy
    z = ((atom & 31) >> 2) + oz - 1
    within = (z >= 0) & (z <= 7)
    top = jnp.where(z > 7, 1, 0)
    side = (col == 0) | (col == 5)
    face = 192 + top * 16 + (col - 1) * 4
    edge = 224 + (top * 2 + jnp.where(col == 5, 1, 0)) * 4
    row = jnp.where(within, col * 32 + z * 4, jnp.where(side, edge, face)) + j
    plane = jnp.where(ox == 1, 0, jnp.where(ox == 0, buffer_of[0], buffer_of[2]))
    cand_ref[...] = (plane * ROWS + row).astype(F32)
    dense_rows[...] = dist[0].reshape(128, slot_count)
    picked[...] = jnp.zeros((128, 128), F32)

    def pick(r, carry):
        q = flag_ids[r]
        picked[pl.ds(r, 1), 0:slot_count] = dense_rows[pl.ds(q, 1), :]
        picked[pl.ds(r, 1), slot_count : 2 * slot_count] = cand_ref[pl.ds(q, 1), :]
        return carry

    lax.fori_loop(0, flags, pick, 0, unroll=8)
    turned = picked[...].T
    half_cut = 0.5 * cutoff_of(turned[0:slot_count])
    cand = turned[slot_count : 2 * slot_count]
    lanes = iota((slot_count, n_buf * ROWS), 1).astype(F32)
    for r in range(flags):
        chosen[slot_count * r : slot_count * (r + 1), :] = jnp.where(
            cand[:, r : r + 1] == lanes, 1.0, 0.0
        ).astype(BF16)
    if inside:
        model_copies[0].wait_recv()
        model_copies[1].wait_recv()
        for copy in model_copies[3:7]:
            copy.start()
    receive_all(second, near.at[1], corner.at[1])
    state = layer(1, state)
    projected = jnp.dot(state, w_env[...], preferred_element_type=F32).astype(BF16)
    proj_ref[...] = projected
    packs_proj[...] = pack(projected)
    third = copies(2, proj_ref, packs_proj, near_proj, corner_proj)
    send_all(third)
    near_proj[0, 32:160, :] = projected
    if inside:
        model_copies[3].wait_recv()
        model_copies[4].wait_recv()
        model_copies[7].start()
    base = lax.dot_general(
        w_out[...], state, (((1,), (1,)), ((), ())), preferred_element_type=F32
    )
    receive_all(third, near_proj, corner_proj)
    planes = near_proj[...].reshape(n_buf * ROWS, near_proj.shape[-1])
    for r0 in range(0, flags, 8):
        nearby = jnp.dot(
            chosen[slot_count * r0 : slot_count * (r0 + 8), :], planes, preferred_element_type=F32
        )
        for r in range(r0, r0 + 8):
            environ[slot_count * r : slot_count * (r + 1), :] = (
                half_cut[:, r : r + 1] * nearby[slot_count * (r - r0) : slot_count * (r - r0 + 1)]
            ).astype(BF16)

    if inside:
        for copy in (model_copies[2], *model_copies[5:]):
            copy.wait_recv()
    lane = iota(base.shape, 1)

    def correct(r, forces):
        p = owner[r]
        rows = environ[pl.ds(pl.multiple_of(r * slot_count, slot_count), slot_count), :]
        half = jnp.dot(rows, models[p, 0:128, :], preferred_element_type=F32)
        hidden = half + half * jnp.tanh(half)
        pooled = (jnp.sum(hidden, axis=0, keepdims=True) * (1.0 / slot_count)).astype(BF16)
        terms = pooled.astype(F32) * (models[p, 128:131, :] if inside else head[p]).astype(F32)
        force = jnp.sum(terms, axis=1, keepdims=True)
        live = jnp.where(r < flag_count[0], 1.0, 0.0)
        return forces + jnp.where(lane == flag_ids[r], force * live, 0.0)

    forces = lax.fori_loop(0, flags, correct, base, unroll=8)
    for y in range(out.shape[2]):
        out[:, 0, y, :] = forces[:, 32 * y : 32 * (y + 1)]
    sent_all(first)
    sent_all(second)
    sent_all(third)
    for copy in model_copies:
        copy.wait_send()


def per_device(
    features,
    neighbour_code,
    distance,
    w_message,
    w_update,
    norm_gain,
    w_env,
    w_out,
    w_first,
    w_head,
    flag_ids,
    flag_owner,
    flag_count,
):
    sizes = tuple(lax.axis_size(name) for name in ("gx", "gy", "gz"))
    n_buf = max(plane_buffers(sizes[0])) + 1
    feature_width = features.shape[-1]
    env_width = w_env.shape[-1]
    message_count = len(messages(sizes[0]))
    local_ids = flag_ids.reshape(-1)
    owner = flag_owner.reshape(-1)
    flags = local_ids.shape[0]
    slot_count = distance.shape[-1]
    inside = sizes[:2] == (2, 4)
    if inside:
        models_shape = (8, 144, w_first.shape[-1])
    else:
        w_first = lax.all_gather(w_first[0], ("gx", "gy"), axis=0)[owner]
        w_head = lax.all_gather(w_head[0], ("gx", "gy"), axis=0)[owner]
        owner = jnp.arange(flags, dtype=jnp.int32)
        models_shape = w_first.shape

    vmem = pl.BlockSpec(memory_space=pltpu.VMEM)
    smem = pl.BlockSpec(memory_space=pltpu.SMEM)
    anywhere = pl.BlockSpec(memory_space=pl.ANY)
    return pl.pallas_call(
        functools.partial(force_kernel, sizes, inside),
        out_shape=jax.ShapeDtypeStruct((3,) + features.shape[:3], F32),
        in_specs=[smem] * 3 + [anywhere] * 7 + [vmem] * 3,
        out_specs=vmem,
        scratch_shapes=[
            pltpu.VMEM(features.shape, BF16),
            pltpu.VMEM(neighbour_code.shape, jnp.int32),
            pltpu.VMEM(distance.shape, F32),
            pltpu.VMEM(w_message.shape, BF16),
            pltpu.VMEM(w_update.shape, BF16),
            pltpu.VMEM(w_env.shape, BF16),
            pltpu.VMEM(models_shape, BF16),
            pltpu.VMEM((NRB * 128, n_buf * ROWS), BF16),
            pltpu.VMEM((128, 128), F32),
            pltpu.VMEM((216, 128), F32),
            pltpu.VMEM((ROWS, 128), jnp.int32),
            pltpu.VMEM((2, n_buf, ROWS, feature_width), BF16),
            pltpu.VMEM((n_buf, ROWS, env_width), BF16),
            pltpu.VMEM((2, n_buf, 4, 16, feature_width), BF16),
            pltpu.VMEM((n_buf, 4, 16, env_width), BF16),
            pltpu.VMEM((2, 96, feature_width), BF16),
            pltpu.VMEM((96, env_width), BF16),
            pltpu.VMEM((2, 128, feature_width), BF16),
            pltpu.VMEM((128, env_width), BF16),
            pltpu.VMEM((128, slot_count), F32),
            pltpu.VMEM((128, slot_count), F32),
            pltpu.VMEM((128, 128), F32),
            pltpu.VMEM((flags * slot_count, env_width), BF16),
            pltpu.VMEM((flags * slot_count, n_buf * ROWS), BF16),
            pltpu.SemaphoreType.DMA((3, message_count)),
            pltpu.SemaphoreType.DMA((3, message_count)),
            pltpu.SemaphoreType.DMA((8,)),
            pltpu.SemaphoreType.DMA((8,)),
            pltpu.SemaphoreType.DMA((7,)),
        ],
        compiler_params=pltpu.CompilerParams(
            collective_id=0, has_side_effects=True, vmem_limit_bytes=56 * 1024 * 1024
        ),
        cost_estimate=pl.CostEstimate(
            flops=2 * 10**9, bytes_accessed=4 * 10**6, transcendentals=3 * 10**6
        ),
        name="forces",
    )(
        local_ids,
        owner,
        flag_count.reshape(-1),
        features,
        neighbour_code,
        distance,
        w_message,
        w_update,
        w_env,
        w_first,
        norm_gain,
        w_out,
        w_head,
    )


def solution(mesh):
    placed = (
        P("gx", "gy", "gz", None),
        P("gx", "gy", "gz", None),
        P("gx", "gy", "gz", None),
        P(),
        P(),
        P(),
        P(),
        P(),
        P(("gx", "gy"), None, None),
        P(("gx", "gy"), None, None),
        P("gx", "gy", "gz", None),
        P("gx", "gy", "gz", None, None),
        P("gx", "gy", "gz"),
    )
    return jax.shard_map(
        per_device, mesh=mesh, in_specs=placed, out_specs=P(None, "gx", "gy", "gz"), check_vma=False
    )
```

```python
import functools

import jax
import jax.numpy as jnp
from jax import lax
from jax.experimental import pallas as pl
from jax.experimental.pallas import tpu as pltpu
from jax.sharding import PartitionSpec as P

M = 4
NRB = 8
L = 2
ROWS = 256
F32 = jnp.float32
BF16 = jnp.bfloat16
MESH = pl.DeviceIdType.MESH


def iota(shape, dim):
    return lax.broadcasted_iota(jnp.int32, shape, dim)


def plane_buffers(n_gx):
    return (1, 0, 1) if n_gx == 2 else (1, 0, 2)


def messages(n_gx):
    steps_x = (1, 0) if n_gx == 2 else (1, -1, 0)
    return [
        (dx, dy, dz)
        for dx in steps_x
        for dy in (0, 1, -1)
        for dz in (0, 1, -1)
        if (dx, dy, dz) != (0, 0, 0)
    ]


def cutoff_of(distance):
    half = distance * (jnp.pi / 10.0)
    sq = half * half
    term = -1.0 / 87178291200.0
    for coef in (1 / 479001600.0, -1 / 3628800.0, 1 / 40320.0, -1 / 720.0, 1 / 24.0, -0.5, 1.0):
        term = term * sq + coef
    return term * term


def face_selector():
    row = iota((96, 128), 0)
    atom = iota((96, 128), 1)
    part = row >> 4
    y = (row & 15) >> 2
    j = row & 3
    g = part - 2
    corner_y = jnp.where((g & 1) == 0, 3, 0)
    corner_z = jnp.where(g < 2, 28, 0)
    corner = jnp.where(y == g, corner_y * 32 + corner_z + j, -1)
    target = jnp.where(part == 0, y * 32 + j, jnp.where(part == 1, y * 32 + 28 + j, corner))
    return jnp.where(atom == target, 1.0, 0.0).astype(BF16)


def candidate_offsets():
    row = iota((ROWS, 128), 0)
    atom = iota((ROWS, 128), 1)
    own_y = atom >> 5
    own_z = (atom & 31) >> 2
    tail = row - 192
    group = (row & 15) >> 2
    col_tail = jnp.where(tail < 32, group + 1, jnp.where((group & 1) == 0, 0, 5))
    col_tail = jnp.where(tail < 48, col_tail, -20)
    z_tail = jnp.where(tail < 16, -1, jnp.where(tail < 32, 8, jnp.where(group < 2, -1, 8)))
    col = jnp.where(row < 192, row >> 5, col_tail)
    z = jnp.where(row < 192, (row & 31) >> 2, z_tail)
    oy = col - own_y
    oz = z - own_z + 1
    good = (oy >= 0) & (oy <= 2) & (oz >= 0) & (oz <= 2)
    return jnp.where(good, oy * 3 + oz, -1)


def force_kernel(
    sizes,
    inside,
    flag_ids,
    owner,
    flag_count,
    feat_hbm,
    code_hbm,
    dist_hbm,
    wm_hbm,
    wu_hbm,
    w_env_hbm,
    first_hbm,
    gain,
    w_out,
    head,
    out,
    feat,
    code,
    dist,
    wm,
    w_update,
    w_env,
    models,
    weights,
    slots,
    dcode,
    offsets,
    near,
    near_proj,
    corner,
    corner_proj,
    packs,
    packs_proj,
    state_ref,
    proj_ref,
    cand_ref,
    dense_rows,
    picked,
    environ,
    chosen,
    send_sem,
    recv_sem,
    model_send,
    model_recv,
    load_sem,
):
    n_gx, n_gy, n_gz = sizes
    buffer_of = plane_buffers(n_gx)
    n_buf = max(buffer_of) + 1
    todo = messages(n_gx)
    me = (lax.axis_index("gx"), lax.axis_index("gy"), lax.axis_index("gz"))

    def target(step):
        return (
            lax.rem(me[0] + step[0] + n_gx, n_gx),
            lax.rem(me[1] + step[1] + n_gy, n_gy),
            me[2] + step[2],
        )

    def along_z(dz, act):
        if dz == 0:
            act()
        elif dz > 0:
            pl.when(me[2] < n_gz - 1)(act)
        else:
            pl.when(me[2] > 0)(act)

    def load(index, source, held):
        copy = pltpu.make_async_copy(source, held, load_sem.at[index])
        copy.start()
        return copy

    loads = [
        load(index, source, held)
        for index, (source, held) in enumerate(
            ((feat_hbm, feat), (code_hbm, code), (dist_hbm, dist))
        )
    ]
    mine = me[0] * n_gy + me[1]
    if inside:
        first_load = load(3, first_hbm.at[0], models.at[mine, pl.ds(0, 128)])
    else:
        first_load = load(3, first_hbm, models)
    late_loads = [
        load(4 + index, source, held)
        for index, (source, held) in enumerate(
            ((wm_hbm, wm), (wu_hbm, w_update), (w_env_hbm, w_env))
        )
    ]
    if inside:
        models[pl.ds(mine, 1), 128:144, :] = jnp.zeros((1, 16, models.shape[-1]), BF16)
        models[pl.ds(mine, 1), 128:131, :] = head[...]

    for b in range(n_buf):
        for e in range(2):
            near[e, b, 192:256, :] = jnp.zeros((64, near.shape[-1]), BF16)
        near_proj[b, 192:256, :] = jnp.zeros((64, near_proj.shape[-1]), BF16)
    corner[...] = jnp.zeros(corner.shape, BF16)
    corner_proj[...] = jnp.zeros(corner_proj.shape, BF16)

    barrier = pltpu.get_barrier_semaphore()
    for step in todo:

        def greet(step=step):
            pl.semaphore_signal(barrier, inc=1, device_id=target(step), device_id_type=MESH)

        along_z(step[2], greet)

    if inside:
        for dx in range(2):
            pl.semaphore_signal(
                barrier, inc=1, device_id=target((dx, 2, 0)), device_id_type=MESH
            )

    selector = face_selector()

    def copies(e, source, packed, plane, corners):
        made = []
        for index, (dx, dy, dz) in enumerate(todo):
            b = 0 if dx == 0 else buffer_of[0 if dx > 0 else 2]
            if dz == 0:
                if dy == 0:
                    src, dst = source, plane.at[b, pl.ds(32, 128)]
                elif dy > 0:
                    src, dst = source.at[pl.ds(96, 32)], plane.at[b, pl.ds(0, 32)]
                else:
                    src, dst = source.at[pl.ds(0, 32)], plane.at[b, pl.ds(160, 32)]
            elif dy == 0:
                src = packed.at[pl.ds(16 if dz > 0 else 0, 16)]
                dst = plane.at[b, pl.ds(192 if dz > 0 else 208, 16)]
            else:
                g = (0 if dz > 0 else 2) + (0 if dy > 0 else 1)
                src, dst = packed.at[pl.ds(32 + 16 * g, 16)], corners.at[b, g]
            made.append(
                pltpu.make_async_remote_copy(
                    src_ref=src,
                    dst_ref=dst,
                    send_sem=send_sem.at[e, index],
                    recv_sem=recv_sem.at[e, index],
                    device_id=target((dx, dy, dz)),
                    device_id_type=MESH,
                )
            )
        return made

    def send_all(made):
        for step, copy in zip(todo, made):
            along_z(step[2], copy.start)

    def receive(made, plane, corners, b):
        for step, copy in zip(todo, made):
            if (0 if step[0] == 0 else buffer_of[0 if step[0] > 0 else 2]) == b:
                along_z(-step[2], copy.wait_recv)
        tile = corners[b, 0].astype(F32)
        for g in range(1, 4):
            tile = tile + corners[b, g].astype(F32)
        plane[b, 224:240, :] = tile.astype(BF16)

    def sent_all(made):
        for step, copy in zip(todo, made):
            along_z(step[2], copy.wait_send)

    shift_y, shift_x, sibling = (
        (lax.rem(me[0] + 1, n_gx), me[1]),
        (me[0], lax.rem(me[1] + 2, n_gy)),
        (me[0], me[1] + 1 - 2 * lax.rem(me[1], 2)),
    )

    def model_copy(index, shard, rows, to):
        part = models.at[shard[0] * n_gy + shard[1], pl.ds(*rows)]
        return pltpu.make_async_remote_copy(
            src_ref=part,
            dst_ref=part,
            send_sem=model_send.at[index],
            recv_sem=model_recv.at[index],
            device_id=(to[0], to[1], me[2]),
            device_id_type=MESH,
        )

    whole_shard = (0, 144)
    model_copies = [
        model_copy(0, me, whole_shard, shift_y),
        model_copy(1, me, whole_shard, shift_x),
        model_copy(2, me, whole_shard, sibling),
        model_copy(3, shift_x, (0, 64), shift_y),
        model_copy(4, shift_y, (64, 80), shift_x),
        model_copy(5, shift_y, whole_shard, sibling),
        model_copy(6, shift_x, whole_shard, sibling),
        model_copy(7, (shift_y[0], shift_x[1]), whole_shard, sibling),
    ] if inside else []

    def pack(state):
        return jnp.dot(selector, state, preferred_element_type=F32).astype(BF16)

    loads[0].wait()
    state = feat[0].reshape(128, feat.shape[-1])
    state_ref[0] = state
    packs[0] = pack(state)
    near[0, 0, 32:160, :] = state

    both = (n_buf) * 3
    here = both - 1 + (2 if inside else 0)
    up = jnp.where(me[2] < n_gz - 1, both, 0)
    down = jnp.where(me[2] > 0, both, 0)
    pl.semaphore_wait(barrier, here + up + down)

    first = copies(0, state_ref.at[0], packs.at[0], near.at[0], corner.at[0])
    send_all(first)
    first_load.wait()
    for copy in model_copies[:3]:
        copy.start()

    loads[1].wait()
    loads[2].wait()
    slot_count = code.shape[-1]
    both_rows = jnp.concatenate(
        [dist[0].reshape(128, slot_count), code[0].reshape(128, slot_count).astype(F32)], axis=1
    )
    slots[...] = both_rows.T
    offsets[...] = candidate_offsets()
    for ox in range(3):
        row = iota((72, 128), 0)
        wanted = (((row >> 3) + 9 * ox) * 4 + (row & 3)).astype(F32)

        def put(s, held):
            named = slots[pl.ds(slot_count + s, 1), :]
            return jnp.where(named == wanted, slots[pl.ds(s, 1), :], held)

        dcode[pl.ds(72 * ox, 72), :] = lax.fori_loop(
            0, slot_count, put, jnp.full((72, 128), -1.0, F32), unroll=8
        )

    for b in range(n_buf):
        for half in range(2):
            where_from = offsets[128 * half : 128 * (half + 1), :]
            parts = []
            for ox in range(3):
                if buffer_of[ox] != b:
                    continue
                dense = jnp.full((128, 128), -1.0, F32)
                for p in range(9):
                    rows = dcode[pl.ds((ox * 9 + p) * 8, 8), :]
                    rows = jnp.broadcast_to(rows[None], (16, 8, 128)).reshape(128, 128)
                    dense = jnp.where(where_from == p, rows, dense)
                dense = dense.T
                parts.append((dense, jnp.where(dense > 0.0, cutoff_of(dense), 0.0)))
            for k in range(NRB):
                total = None
                for dense, cut in parts:
                    gap = dense - (0.8 + k * (4.0 / (NRB - 1)))
                    basis = jnp.exp(-2.0 * (gap * gap)) * cut
                    total = basis if total is None else total + basis
                weights[128 * k : 128 * (k + 1), 256 * b + 128 * half : 256 * b + 128 * (half + 1)] = (
                    total.astype(BF16)
                )

    def layer(l, state, made):
        width = state.shape[-1]
        summed = jnp.zeros((NRB * 128, width), F32)
        for b in range(n_buf):
            receive(made, near.at[l], corner.at[l], b)
            summed = summed + jnp.dot(
                weights[:, ROWS * b : ROWS * (b + 1)], near[l, b], preferred_element_type=F32
            )
        summed = summed.astype(BF16)
        summed = jnp.concatenate([summed[128 * k : 128 * (k + 1)] for k in range(NRB)], axis=1)
        half = 0.5 * jnp.dot(summed, wm[l], preferred_element_type=F32)
        active = (half + half * jnp.tanh(half)).astype(BF16)
        residual = state.astype(F32) + jnp.dot(active, w_update[l], preferred_element_type=F32)
        inv_rms = lax.rsqrt(jnp.mean(residual * residual, axis=-1, keepdims=True) + 1e-06)
        return (residual * inv_rms * gain[l : l + 1, :]).astype(BF16)

    for copy in late_loads:
        copy.wait()
    state = layer(0, state, first)
    state_ref[1] = state
    packs[1] = pack(state)
    second = copies(1, state_ref.at[1], packs.at[1], near.at[1], corner.at[1])
    send_all(second)
    near[1, 0, 32:160, :] = state
    flags = flag_ids.shape[0]
    codes = code[0].reshape(128, slot_count)
    atom = iota((128, slot_count), 0)
    o = lax.div(codes, M)
    j = codes & 3
    ox = lax.div(o, 9)
    oy = lax.rem(lax.div(o, 3), 3)
    oz = lax.rem(o, 3)
    col = (atom >> 5) + oy
    z = ((atom & 31) >> 2) + oz - 1
    within = (z >= 0) & (z <= 7)
    top = jnp.where(z > 7, 1, 0)
    side = (col == 0) | (col == 5)
    face = 192 + top * 16 + (col - 1) * 4
    edge = 224 + (top * 2 + jnp.where(col == 5, 1, 0)) * 4
    row = jnp.where(within, col * 32 + z * 4, jnp.where(side, edge, face)) + j
    plane = jnp.where(ox == 1, 0, jnp.where(ox == 0, buffer_of[0], buffer_of[2]))
    cand_ref[...] = (plane * ROWS + row).astype(F32)
    dense_rows[...] = dist[0].reshape(128, slot_count)
    picked[...] = jnp.zeros((128, 128), F32)

    def pick(r, carry):
        q = flag_ids[r]
        picked[pl.ds(r, 1), 0:slot_count] = dense_rows[pl.ds(q, 1), :]
        picked[pl.ds(r, 1), slot_count : 2 * slot_count] = cand_ref[pl.ds(q, 1), :]
        return carry

    lax.fori_loop(0, flags, pick, 0, unroll=8)
    turned = picked[...].T
    half_cut = 0.5 * cutoff_of(turned[0:slot_count])
    cand = turned[slot_count : 2 * slot_count]
    lanes = iota((slot_count, n_buf * ROWS), 1).astype(F32)
    for r in range(flags):
        chosen[slot_count * r : slot_count * (r + 1), :] = jnp.where(
            cand[:, r : r + 1] == lanes, 1.0, 0.0
        ).astype(BF16)
    if inside:
        model_copies[0].wait_recv()
        model_copies[1].wait_recv()
        for copy in model_copies[3:7]:
            copy.start()
    state = layer(1, state, second)
    projected = jnp.dot(state, w_env[...], preferred_element_type=F32).astype(BF16)
    proj_ref[...] = projected
    packs_proj[...] = pack(projected)
    third = copies(2, proj_ref, packs_proj, near_proj, corner_proj)
    send_all(third)
    near_proj[0, 32:160, :] = projected
    if inside:
        model_copies[3].wait_recv()
        model_copies[4].wait_recv()
        model_copies[7].start()
    base = lax.dot_general(
        w_out[...], state, (((1,), (1,)), ((), ())), preferred_element_type=F32
    )
    for b in range(n_buf):
        receive(third, near_proj, corner_proj, b)
    planes = near_proj[...].reshape(n_buf * ROWS, near_proj.shape[-1])
    for r0 in range(0, flags, 8):
        nearby = jnp.dot(
            chosen[slot_count * r0 : slot_count * (r0 + 8), :], planes, preferred_element_type=F32
        )
        for r in range(r0, r0 + 8):
            environ[slot_count * r : slot_count * (r + 1), :] = (
                half_cut[:, r : r + 1] * nearby[slot_count * (r - r0) : slot_count * (r - r0 + 1)]
            ).astype(BF16)

    if inside:
        for copy in (model_copies[2], *model_copies[5:]):
            copy.wait_recv()
    lane = iota(base.shape, 1)

    def correct(r, forces):
        p = owner[r]
        rows = environ[pl.ds(pl.multiple_of(r * slot_count, slot_count), slot_count), :]
        half = jnp.dot(rows, models[p, 0:128, :], preferred_element_type=F32)
        hidden = half + half * jnp.tanh(half)
        pooled = (jnp.sum(hidden, axis=0, keepdims=True) * (1.0 / slot_count)).astype(BF16)
        terms = pooled.astype(F32) * (models[p, 128:131, :] if inside else head[p]).astype(F32)
        force = jnp.sum(terms, axis=1, keepdims=True)
        live = jnp.where(r < flag_count[0], 1.0, 0.0)
        return forces + jnp.where(lane == flag_ids[r], force * live, 0.0)

    forces = lax.fori_loop(0, flags, correct, base, unroll=8)
    for y in range(out.shape[2]):
        out[:, 0, y, :] = forces[:, 32 * y : 32 * (y + 1)]
    sent_all(first)
    sent_all(second)
    sent_all(third)
    for copy in model_copies:
        copy.wait_send()


def per_device(
    features,
    neighbour_code,
    distance,
    w_message,
    w_update,
    norm_gain,
    w_env,
    w_out,
    w_first,
    w_head,
    flag_ids,
    flag_owner,
    flag_count,
):
    sizes = tuple(lax.axis_size(name) for name in ("gx", "gy", "gz"))
    n_buf = max(plane_buffers(sizes[0])) + 1
    feature_width = features.shape[-1]
    env_width = w_env.shape[-1]
    message_count = len(messages(sizes[0]))
    local_ids = flag_ids.reshape(-1)
    owner = flag_owner.reshape(-1)
    flags = local_ids.shape[0]
    slot_count = distance.shape[-1]
    inside = sizes[:2] == (2, 4)
    if inside:
        models_shape = (8, 144, w_first.shape[-1])
    else:
        w_first = lax.all_gather(w_first[0], ("gx", "gy"), axis=0)[owner]
        w_head = lax.all_gather(w_head[0], ("gx", "gy"), axis=0)[owner]
        owner = jnp.arange(flags, dtype=jnp.int32)
        models_shape = w_first.shape

    vmem = pl.BlockSpec(memory_space=pltpu.VMEM)
    smem = pl.BlockSpec(memory_space=pltpu.SMEM)
    anywhere = pl.BlockSpec(memory_space=pl.ANY)
    return pl.pallas_call(
        functools.partial(force_kernel, sizes, inside),
        out_shape=jax.ShapeDtypeStruct((3,) + features.shape[:3], F32),
        in_specs=[smem] * 3 + [anywhere] * 7 + [vmem] * 3,
        out_specs=vmem,
        scratch_shapes=[
            pltpu.VMEM(features.shape, BF16),
            pltpu.VMEM(neighbour_code.shape, jnp.int32),
            pltpu.VMEM(distance.shape, F32),
            pltpu.VMEM(w_message.shape, BF16),
            pltpu.VMEM(w_update.shape, BF16),
            pltpu.VMEM(w_env.shape, BF16),
            pltpu.VMEM(models_shape, BF16),
            pltpu.VMEM((NRB * 128, n_buf * ROWS), BF16),
            pltpu.VMEM((128, 128), F32),
            pltpu.VMEM((216, 128), F32),
            pltpu.VMEM((ROWS, 128), jnp.int32),
            pltpu.VMEM((2, n_buf, ROWS, feature_width), BF16),
            pltpu.VMEM((n_buf, ROWS, env_width), BF16),
            pltpu.VMEM((2, n_buf, 4, 16, feature_width), BF16),
            pltpu.VMEM((n_buf, 4, 16, env_width), BF16),
            pltpu.VMEM((2, 96, feature_width), BF16),
            pltpu.VMEM((96, env_width), BF16),
            pltpu.VMEM((2, 128, feature_width), BF16),
            pltpu.VMEM((128, env_width), BF16),
            pltpu.VMEM((128, slot_count), F32),
            pltpu.VMEM((128, slot_count), F32),
            pltpu.VMEM((128, 128), F32),
            pltpu.VMEM((flags * slot_count, env_width), BF16),
            pltpu.VMEM((flags * slot_count, n_buf * ROWS), BF16),
            pltpu.SemaphoreType.DMA((3, message_count)),
            pltpu.SemaphoreType.DMA((3, message_count)),
            pltpu.SemaphoreType.DMA((8,)),
            pltpu.SemaphoreType.DMA((8,)),
            pltpu.SemaphoreType.DMA((7,)),
        ],
        compiler_params=pltpu.CompilerParams(
            collective_id=0, has_side_effects=True, vmem_limit_bytes=56 * 1024 * 1024
        ),
        cost_estimate=pl.CostEstimate(
            flops=2 * 10**9, bytes_accessed=4 * 10**6, transcendentals=3 * 10**6
        ),
        name="forces",
    )(
        local_ids,
        owner,
        flag_count.reshape(-1),
        features,
        neighbour_code,
        distance,
        w_message,
        w_update,
        w_env,
        w_first,
        norm_gain,
        w_out,
        w_head,
    )


def solution(mesh):
    placed = (
        P("gx", "gy", "gz", None),
        P("gx", "gy", "gz", None),
        P("gx", "gy", "gz", None),
        P(),
        P(),
        P(),
        P(),
        P(),
        P(("gx", "gy"), None, None),
        P(("gx", "gy"), None, None),
        P("gx", "gy", "gz", None),
        P("gx", "gy", "gz", None, None),
        P("gx", "gy", "gz"),
    )
    return jax.shard_map(
        per_device, mesh=mesh, in_specs=placed, out_specs=P(None, "gx", "gy", "gz"), check_vma=False
    )
```
